256 devices in a mesh: pair: 16 (over x_lo, y, core), grp: 16 (over z, x_hi).
Axes of the slice: x: 4 (x_hi: 2, x_lo: 2; x = x_hi * 2 + x_lo), y: 4, z: 8, core: 2. Of those that a mesh axis runs over, the one named last changes fastest.
Arguments:
- amplitudes: float32 [48, 48, 4096], P('pair', 'grp'), may hold values from -6 to 6
- integrals: float32 [4096, 20480], P('pair', 'grp'), may hold values from -0.125 to 0.125
- occ_start: int32 [8], replicated, may hold values from 0 to 2160, as said below
- vir_start: int32 [8], replicated, may hold values from 0 to 3840, as said below
- block_mask: int32 [8, 8], replicated, may hold values 0 or 1
- occ_energy: float32 [48, 48], P('pair', 'grp'), may hold values from -1.5 to -0.5
- vir_energy: float32 [20480], replicated, may hold values from 0.4 to 2.5
Outputs:
- update: float32 [48, 48, 20480], P('pair', 'grp')
The draws below stay inside these ranges and needn't reach their ends.
Inputs may be any that keep to these rules, and one draw needn't show every extreme that they name: `occ_start`: strictly rising; the first entry is 0; the last block holds 144 pairs. `vir_start`: strictly rising; the first entry is 0; the last block holds 256 pairs.
All inputs are finite; a program needn't handle non-finite values.
Results may differ from the reference program's by a relative error of at most 0.00007.
Values sent between devices are 32-bit elements; how exact they have to be, the bound alone decides.
No kernel may reach another device: no remote copies, remote signals or barrier semaphores. Data moves between devices by JAX's collectives and lax.ppermute only.
A program may use at most 128 MiB of HBM per device.

```python
import jax
import jax.numpy as jnp
from jax import lax

VPC = 4096
VPO = 20480
NIRO = 8
NIRV = 8
OPO = 48
OPI = 48


def cut_points(key, total, count):
    last_start = total - total // (2 * count)
    picks = jax.random.permutation(key, last_start - 1)[:count - 2] + 1
    inner_cuts = jnp.sort(picks).astype(jnp.int32)
    return jnp.concatenate([jnp.zeros((1,), jnp.int32), inner_cuts, jnp.full((1,), last_start, jnp.int32)])


def draw_occ_start(key, part):
    key = jax.random.fold_in(key, 11)
    return cut_points(key, OPO * OPI, NIRO)


def draw_vir_start(key, part):
    key = jax.random.fold_in(key, 23)
    return cut_points(key, VPC, NIRV)


def touch_ends(result, stream_key, least, high):
    index_at = [jax.random.randint(jax.random.fold_in(stream_key, axis), (), 0, length) for axis, length in enumerate(result.shape)]
    main_axis = result.shape.index(max(result.shape))
    next_to = index_at[:main_axis] + [(index_at[main_axis] + 1) % result.shape[main_axis]] + index_at[main_axis + 1:]
    return result.at[tuple(index_at)].set(least).at[tuple(next_to)].set(high)


def levels(stream_key, shape, shards, low, largest):
    level = 1.0
    for position, parts in shards:
        steps = jax.random.uniform(jax.random.fold_in(jax.random.fold_in(stream_key, 6), position), (parts,), jnp.float32, low / len(shards), largest / len(shards))
        level = level * jnp.repeat(jnp.exp(steps), shape[position] // parts).reshape((-1,) + (1,) * (len(shape) - 1 - position))
    return level


def normal_values(stream_key, extent, scale, bound, pieces=(), kind=jnp.bfloat16):
    result = scale * jax.random.normal(stream_key, extent, jnp.float32)
    if pieces:
        result = result * levels(stream_key, extent, pieces, -0.22, 0.18)
    return jnp.clip(result, -bound, bound).astype(kind)


def setup_inputs(seed: int = 0) -> dict:
    splits = jax.random.split(jax.random.key(seed), 8)
    return {
        "amplitudes": normal_values(splits[0], (OPO, OPI, VPC), 1.0, 6.0, ((0, 16), (1, 16)), jnp.float32),
        "integrals": normal_values(splits[1], (VPC, VPO), (VPC // 2) ** -0.5, 0.125, ((0, 16), (1, 16)), jnp.float32),
        "occ_start": draw_occ_start(jax.random.fold_in(splits[7], 71), 0),
        "vir_start": draw_vir_start(jax.random.fold_in(splits[7], 71), 0),
        "block_mask": touch_ends((jax.random.randint(splits[4], (NIRO, NIRV), 0, 4) < 3).astype(jnp.int32), jax.random.fold_in(splits[4], 1), 0, 1),
        "occ_energy": jnp.clip(-1.5 + 1.0 * jax.random.uniform(splits[5], (OPO, OPI), jnp.float32) ** levels(splits[5], (OPO, OPI), ((0, 16), (1, 16)), -0.2, 0.2), -1.5, -0.5),
        "vir_energy": jnp.clip(jax.random.uniform(splits[6], (VPO,), jnp.float32, 0.4, 2.5), 0.4, 2.5),
    }


def block_ids(index, starts):
    return jnp.sum((index[:, None] >= starts[None, :]).astype(jnp.int32), axis=1) - 1


def reference(amplitudes, integrals, occ_start, vir_start, block_mask, occ_energy, vir_energy):
    row_ids = jnp.arange(OPO * OPI, dtype=jnp.int32)
    col_ids = jnp.arange(VPC, dtype=jnp.int32)
    row_block = block_ids(row_ids, occ_start)
    col_block = block_ids(col_ids, vir_start)
    keep = block_mask[row_block[:, None], col_block[None, :]].astype(jnp.float32)
    masked = amplitudes.reshape(OPO * OPI, VPC) * keep
    ladder = jnp.dot(masked, integrals, precision=lax.Precision.HIGHEST, preferred_element_type=jnp.float32)
    denom = occ_energy.reshape(OPO * OPI)[:, None] - vir_energy[None, :]
    return (ladder / denom).reshape(OPO, OPI, VPO)
```

```python
import jax
import jax.numpy as jnp
from jax import lax
from jax.experimental import pallas as pl
from jax.experimental.pallas import tpu as pltpu
from jax.sharding import Mesh, PartitionSpec as P

AXES = ("xl", "y", "core", "z", "xh")
SIZES = (2, 4, 2, 8, 2)
PAIR, GRP = ("xl", "y", "core"), ("z", "xh")
NZ = 8


def swap(x, axes, bits):
    names = axes if isinstance(axes, tuple) else (axes,)
    n = 1
    for a in names:
        n *= SIZES[AXES.index(a)]
    return lax.ppermute(x, axes, [(i, i ^ bits) for i in range(n)])


def along_z(x, d):
    return lax.ppermute(x, "z", [(i, (i + d) % NZ) for i in range(NZ)])


def mask_kernel(occ_ref, vir_ref, mask_ref, a_ref, out_ref, held):
    xl, y, core = lax.axis_index("xl"), lax.axis_index("y"), lax.axis_index("core")
    z, xh = lax.axis_index("z"), lax.axis_index("xh")
    no, ni, width = a_ref.shape
    blocks = vir_ref.shape[0]
    part = width // 16
    col = lax.broadcasted_iota(jnp.int32, (1, width), 1)
    block = jnp.full((1, width), -1, jnp.int32)
    for s in range(blocks):
        block = block + (col >= vir_ref[s]).astype(jnp.int32)
    for oo in range(no):
        for ii in range(ni):
            o = ((xl * 4 + y) * 2 + core) * no + oo
            row = o * (ni * 16) + (z * 2 + xh) * ni + ii
            row_block = jnp.int32(-1)
            for s in range(occ_ref.shape[0]):
                row_block = row_block + (row >= occ_ref[s]).astype(jnp.int32)
            keep = jnp.zeros((1, width), jnp.float32)
            for v in range(blocks):
                keep = jnp.where(block == v, mask_ref[row_block, v].astype(jnp.float32), keep)
            held[oo * ni + ii : oo * ni + ii + 1, :] = a_ref[oo, ii : ii + 1, :] * keep
    for e in range(4):
        for dc in range(2):
            for dx in range(2):
                p = ((xl ^ dx) * 4 + (y ^ e)) * 2 + (core ^ dc)
                out_ref[dc, e, :, dx * part : (dx + 1) * part] = held[
                    :, pl.ds(pl.multiple_of(p * part, part), part)
                ]


def mask_rows(amplitudes, occ_start, vir_start, block_mask):
    no, ni, width = amplitudes.shape
    smem = pl.BlockSpec(memory_space=pltpu.SMEM)
    vmem = pl.BlockSpec(memory_space=pltpu.VMEM)
    return pl.pallas_call(
        mask_kernel,
        out_shape=jax.ShapeDtypeStruct((2, 4, no * ni, width // 8), jnp.float32),
        in_specs=[smem, smem, smem, vmem],
        out_specs=vmem,
        scratch_shapes=[pltpu.VMEM((no * ni, width), jnp.float32)],
    )(occ_start, vir_start, block_mask, amplitudes)


def scale_kernel(*refs):
    parts, (occ_ref, vir_ref, out_ref) = refs[:NZ], refs[NZ:]
    z, xh = lax.axis_index("z"), lax.axis_index("xh")
    width = parts[0].shape[2] // 2
    for d in range(NZ):
        for h in range(2):
            where = (lax.rem(z + d, NZ) * 2 + (xh ^ h)) * width
            cols = pl.ds(pl.multiple_of(where, width), width)
            for oo in range(out_ref.shape[0]):
                denom = occ_ref[oo] - vir_ref[:, cols]
                out_ref[oo, :, cols] = parts[d][oo, :, h * width : (h + 1) * width] / denom


def scale(parts, occ_energy, vir_energy):
    no, ni, width = parts[0].shape
    vmem = pl.BlockSpec(memory_space=pltpu.VMEM)
    return pl.pallas_call(
        scale_kernel,
        out_shape=jax.ShapeDtypeStruct((no, ni, width * NZ), jnp.float32),
        in_specs=[vmem] * (NZ + 2),
        out_specs=vmem,
    )(*parts, occ_energy[:, :, None], vir_energy[None, :])


def dot(a, b):
    return jnp.dot(a, b, precision=lax.Precision.HIGH, preferred_element_type=jnp.float32)


def on_device(amplitudes, integrals, occ_start, vir_start, block_mask, occ_energy, vir_energy):
    no, ni, _ = amplitudes.shape
    nr = no * ni
    with jax.named_scope("gather_integrals"):
        b_xl = swap(integrals, "xl", 1)
        b_d = swap(integrals, ("xl", "xh"), 3)
        b_xh = swap(integrals, "xh", 1)
    with jax.named_scope("mask"):
        sends = mask_rows(amplitudes, occ_start, vir_start, block_mask)
    depth = sends.shape[3]
    with jax.named_scope("exchange_amplitudes"):
        pair = jnp.stack([sends[0], swap(sends[1], "core", 1)], axis=1)
        rows = [pair[0]] + [swap(pair[e], "y", e) for e in (1, 2, 3)]
        mine = jnp.stack(rows, axis=1).reshape(8 * nr, depth)
    with jax.named_scope("gather_amplitudes"):
        got = [mine] + [along_z(mine, d) for d in range(1, NZ)]
        flat = jnp.stack([g.reshape(2, 4, nr, depth) for g in got], axis=2)
        flat = flat.reshape(2, 4 * NZ * nr, depth)
    half = depth // 2
    group = NZ * nr

    def block(side, h):
        near, far = ((integrals, b_xl), (b_xh, b_d))[h]
        return dot(flat[side, :, :half], near) + dot(flat[side, :, half:], far)

    sums = []
    for h in range(2):
        with jax.named_scope("product"):
            theirs = block(1, h)
        with jax.named_scope("sum_core"):
            other = swap(theirs, "core", 1)
        with jax.named_scope("product"):
            total = block(0, h)
        with jax.named_scope("sum_core"):
            total = (total + other).reshape(4, group, -1)
        sums.append(total)
    with jax.named_scope("sum_y"):
        r0 = swap(sums[0][1:3], "y", 1)
        r1 = swap(sums[1][2:4], "y", 3)
        s0 = swap(sums[0][3] + r0[1], "y", 3)
        s1 = swap(sums[1][1] + r1[0], "y", 1)
        piece = jnp.concatenate([sums[0][0] + r0[0] + s0, sums[1][0] + r1[1] + s1], axis=1)
    with jax.named_scope("to_owner"):
        piece = piece.reshape(NZ, no, ni, -1)
        parts = [piece[0]] + [along_z(piece[d], NZ - d) for d in range(1, NZ)]
    with jax.named_scope("scale"):
        return scale(parts, occ_energy, vir_energy)


def solution(mesh):
    split = Mesh(mesh.devices.reshape(SIZES), AXES)
    return jax.shard_map(
        on_device,
        mesh=split,
        in_specs=(P(PAIR, GRP, None), P(PAIR, GRP), P(), P(), P(), P(PAIR, GRP), P()),
        out_specs=P(PAIR, GRP, None),
        check_vma=False,
    )
```

```python
import jax
import jax.numpy as jnp
from jax import lax
from jax.experimental import pallas as pl
from jax.experimental.pallas import tpu as pltpu
from jax.sharding import Mesh, PartitionSpec as P

AXES = ("xl", "y", "core", "z", "xh")
SIZES = (2, 4, 2, 8, 2)
PAIR, GRP = ("xl", "y", "core"), ("z", "xh")
NZ = 8
CHEAP = pl.CostEstimate(flops=1000, bytes_accessed=1000, transcendentals=0)
VMEM = pl.BlockSpec(memory_space=pltpu.VMEM)
ANY = pl.BlockSpec(memory_space=pl.ANY)


def call(kernel, out_shape, operands, after=(), scratch=(), mib=8):
    several = isinstance(out_shape, list)

    def body(*refs):
        kernel(*refs[: len(operands)], *refs[len(operands) + len(after) :])

    return pl.pallas_call(
        body,
        out_shape=out_shape,
        in_specs=[VMEM] * len(operands) + [ANY] * len(after),
        out_specs=[VMEM] * len(out_shape) if several else VMEM,
        scratch_shapes=list(scratch),
        cost_estimate=CHEAP,
        compiler_params=pltpu.CompilerParams(vmem_limit_bytes=mib * 2**20),
        name=kernel.__name__,
    )(*operands, *after)


def f32(*shape):
    return jax.ShapeDtypeStruct(shape, jnp.float32)


def swap(x, axes, bits):
    names = axes if isinstance(axes, tuple) else (axes,)
    n = 1
    for a in names:
        n *= SIZES[AXES.index(a)]
    return lax.ppermute(x, axes, [(i, i ^ bits) for i in range(n)])


def along_z(x, d):
    return lax.ppermute(x, "z", [(i, (i + d) % NZ) for i in range(NZ)])


def mask_kernel(occ_ref, vir_ref, mask_ref, a_ref, near_ref, far_ref, held):
    xl, y, core = lax.axis_index("xl"), lax.axis_index("y"), lax.axis_index("core")
    z, xh = lax.axis_index("z"), lax.axis_index("xh")
    no, ni, width = a_ref.shape
    blocks = vir_ref.shape[0]
    part = width // 16
    col = lax.broadcasted_iota(jnp.int32, (1, width), 1)
    block = jnp.full((1, width), -1, jnp.int32)
    for s in range(blocks):
        block = block + (col >= vir_ref[s]).astype(jnp.int32)
    for oo in range(no):
        for ii in range(ni):
            o = ((xl * 4 + y) * 2 + core) * no + oo
            row = o * (ni * 16) + (z * 2 + xh) * ni + ii
            row_block = jnp.int32(-1)
            for s in range(occ_ref.shape[0]):
                row_block = row_block + (row >= occ_ref[s]).astype(jnp.int32)
            keep = jnp.zeros((1, width), jnp.float32)
            for v in range(blocks):
                keep = jnp.where(block == v, mask_ref[row_block, v].astype(jnp.float32), keep)
            held[oo * ni + ii : oo * ni + ii + 1, :] = a_ref[oo, ii : ii + 1, :] * keep
    for e in range(4):
        for dc in range(2):
            for dx in range(2):
                p = ((xl ^ dx) * 4 + (y ^ e)) * 2 + (core ^ dc)
                (near_ref, far_ref)[dc][e, :, dx * part : (dx + 1) * part] = held[
                    :, pl.ds(pl.multiple_of(p * part, part), part)
                ]


def mask_rows(amplitudes, occ_start, vir_start, block_mask):
    no, ni, width = amplitudes.shape
    smem = pl.BlockSpec(memory_space=pltpu.SMEM)
    half = jax.ShapeDtypeStruct((4, no * ni, width // 8), jnp.float32)
    return pl.pallas_call(
        mask_kernel,
        out_shape=[half, half],
        in_specs=[smem, smem, smem, VMEM],
        out_specs=[VMEM, VMEM],
        scratch_shapes=[pltpu.VMEM((no * ni, width), jnp.float32)],
        cost_estimate=CHEAP,
        compiler_params=pltpu.CompilerParams(vmem_limit_bytes=8 * 2**20),
    )(occ_start, vir_start, block_mask, amplitudes)


def by_row_kernel(near_ref, far_ref, *outs):
    for e in range(4):
        outs[e][0] = near_ref[e]
        outs[e][1] = far_ref[e]


def by_row(near, far):
    return call(by_row_kernel, [f32(2, *near.shape[1:])] * 4, (near, far))


def line_up_kernel(*refs):
    rows, out_ref = refs[:4], refs[-1]
    nr = rows[0].shape[1]
    for dc in range(2):
        for e in range(4):
            at = (dc * 4 + e) * nr
            out_ref[at : at + nr, :] = rows[e][dc]


def line_up(rows):
    _, nr, depth = rows[0].shape
    return call(line_up_kernel, f32(8 * nr, depth), rows)


def pair_up_kernel(a, b, c, d, left, right):
    n = a.shape[0]
    left[:n], left[n:] = a[...], b[...]
    right[:n], right[n:] = c[...], d[...]


def pair_up(mine, down1, up1, across):
    n, depth = mine.shape
    return call(pair_up_kernel, [f32(2 * n, depth)] * 2, (mine, down1, mine, up1), (across,))


def pass_on_kernel(two, up1, six, down1, up, down):
    up[0], up[1] = two[...], up1[1]
    down[0], down[1] = six[...], down1[1]


def pass_on(two, up1, six, down1, across):
    return call(pass_on_kernel, [f32(*up1.shape)] * 2, (two, up1, six, down1), (across,))


def order_kernel(*refs):
    own, down1, up1, across, down, up = refs[:6]
    highs, lows, held = (refs[6], refs[8]), (refs[7], refs[9]), refs[10]
    n = own.shape[0]
    nr = n // 8
    source = [(own, 0), (down1, 0), (down, 0), (down, n), (across, 0), (up, n), (up, 0), (up1, 0)]
    for dc in range(2):
        for e in range(4):
            for d, (ref, base) in enumerate(source):
                at = (e * NZ + d) * nr
                where = base + (dc * 4 + e) * nr
                held[at : at + nr, :] = ref[where : where + nr, :]
        value = held[...]
        high = value.astype(jnp.bfloat16)
        highs[dc][...] = high
        lows[dc][...] = (value - high.astype(jnp.float32)).astype(jnp.bfloat16)


def order_rows(*blocks):
    n, depth = blocks[0].shape
    part = jax.ShapeDtypeStruct((4 * n, depth), jnp.bfloat16)
    return call(order_kernel, [part] * 4, blocks, scratch=[pltpu.VMEM((4 * n, depth), jnp.float32)])


def halve_kernel(a, b, first, second):
    n = first.shape[0]
    first[...] = a[:n, :]
    second[...] = b[n:, :]


def halve(a, b, after):
    depth, width = a.shape
    return call(halve_kernel, [f32(depth // 2, width)] * 2, (a, b), after)


def three_passes(high_ref, low_ref, b_refs, cols, b_high, b_low):
    at = 0
    for ref in b_refs:
        value = ref[:, cols]
        high = value.astype(jnp.bfloat16)
        b_high[at : at + ref.shape[0], :] = high
        b_low[at : at + ref.shape[0], :] = (value - high.astype(jnp.float32)).astype(jnp.bfloat16)
        at += ref.shape[0]
    dot = lambda a, b: jnp.dot(a, b, preferred_element_type=jnp.float32)
    small = dot(high_ref[...], b_low[...]) + dot(low_ref[...], b_high[...])
    return small + dot(high_ref[...], b_high[...])


def theirs_kernel(high_ref, low_ref, *refs):
    b_refs, (out_ref, b_high, b_low) = refs[:-3], refs[-3:]
    width = b_high.shape[1]
    for s in range(2):
        cols = slice(s * width, (s + 1) * width)
        out_ref[:, cols] = three_passes(high_ref, low_ref, b_refs, cols, b_high, b_low)


def ours_kernel(high_ref, low_ref, *refs):
    b_refs, other_ref, outs, (b_high, b_low) = refs[:-7], refs[-7], refs[-6:-2], refs[-2:]
    width = b_high.shape[1]
    group = outs[0].shape[0] // 2
    for s in range(2):
        cols = slice(s * width, (s + 1) * width)
        value = three_passes(high_ref, low_ref, b_refs, cols, b_high, b_low) + other_ref[:, cols]
        part = [value[e * group : (e + 1) * group] for e in range(4)]
        send, keep = outs[2 * s], outs[2 * s + 1]
        gone, kept = (((1, 2), (0, 3)), ((2, 3), (0, 1)))[s]
        for k in range(2):
            send[k * group : (k + 1) * group, :] = part[gone[k]]
            keep[k * group : (k + 1) * group, :] = part[kept[k]]


def product(high, low, pieces, other=None, after=()):
    rows, depth = high.shape
    width = pieces[0].shape[1]
    scratch = [pltpu.VMEM((depth, width // 2), jnp.bfloat16)] * 2
    if other is None:
        return call(theirs_kernel, f32(rows, width), (high, low, *pieces), after, scratch, 16)
    outs = [f32(rows // 2, width // 2)] * 4
    return call(ours_kernel, outs, (high, low, *pieces, other), after, scratch, 16)


def middle_kernel(keep_a, got_a, keep_b, got_b, send_a, send_b):
    group = send_a.shape[0]
    send_a[...] = keep_a[group:, :] + got_a[group:, :]
    send_b[...] = keep_b[group:, :] + got_b[:group, :]


def middle(*args, after=()):
    n, width = args[0].shape
    return call(middle_kernel, [f32(n // 2, width)] * 2, args, after)


def finish_kernel(*refs):
    sides, outs = (refs[:3], refs[3:6]), refs[6:]
    own, up1, down1, across, two, six = outs
    group, width = sides[0][2].shape
    nr = group // NZ
    where = [own, (up1, 0), two, (up1, 1), across, (down1, 1), six, (down1, 0)]
    for s, (keep, got, last) in enumerate(sides):
        first = 0 if s == 0 else group
        value = keep[:group, :] + got[first : first + group, :] + last[...]
        for d in range(NZ):
            for j in range(width // 128):
                at = (s * (width // 128) + j) * nr
                tile = value[d * nr : (d + 1) * nr, j * 128 : (j + 1) * 128]
                if isinstance(where[d], tuple):
                    where[d][0][where[d][1], at : at + nr, :] = tile
                else:
                    where[d][at : at + nr, :] = tile


def finish(*args):
    group, width = args[2].shape
    rows = 2 * width // 128 * (group // NZ)
    one, two = f32(rows, 128), f32(2, rows, 128)
    return call(finish_kernel, [one, two, two, one, one, one], args)


def scale_kernel(*refs):
    halves, (occ_ref, vir_ref, out_ref) = (refs[:6], refs[6:12]), refs[12:]
    z, xh = lax.axis_index("z"), lax.axis_index("xh")
    no, ni, _ = out_ref.shape
    nr = no * ni
    tiles = refs[0].shape[0] // nr
    for h, (own, up1, up, across, down, down1) in enumerate(halves):
        source = [own, up1.at[0], up.at[0], up.at[1], across, down.at[1], down.at[0], down1.at[0]]
        for d, ref in enumerate(source):
            start = (lax.rem(z + d, NZ) * 2 + (xh ^ h)) * tiles
            for j in range(tiles):
                cols = pl.ds(pl.multiple_of((start + j) * 128, 128), 128)
                value = ref[j * nr : (j + 1) * nr, :] / (occ_ref[...] - vir_ref[:, cols])
                for oo in range(no):
                    out_ref[oo, :, cols] = value[oo * ni : (oo + 1) * ni]


def scale(near, far, occ_energy, vir_energy):
    no, ni = occ_energy.shape
    operands = (*near, *far, occ_energy.reshape(no * ni, 1), vir_energy[None, :])
    return call(scale_kernel, f32(no, ni, vir_energy.shape[0]), operands)


def on_device(amplitudes, integrals, occ_start, vir_start, block_mask, occ_energy, vir_energy):
    with jax.named_scope("gather_integrals"):
        xl, d = swap(integrals, "xl", 1), swap(integrals, ("xl", "xh"), 3)
    with jax.named_scope("mask"):
        near, far = mask_rows(amplitudes, occ_start, vir_start, block_mask)
    with jax.named_scope("exchange_amplitudes"):
        pair = by_row(near, swap(far, "core", 1))
        rows = [pair[0]] + [swap(pair[e], "y", e) for e in (1, 2, 3)]
        mine = line_up(rows)
    with jax.named_scope("gather_amplitudes"):
        across, down1, up1 = along_z(mine, 4), along_z(mine, 1), along_z(mine, 7)
        pairs = pair_up(mine, down1, up1, across)
        down, up = along_z(pairs[0], 2), along_z(pairs[1], 6)
        ours_high, ours_low, theirs_high, theirs_low = order_rows(mine, down1, up1, across, down, up)
    with jax.named_scope("gather_integrals"):
        first, second = halve(xl, d, after=(pairs[0],))
        first, second = swap(first, ("xl", "xh"), 3), swap(second, "xl", 1)
    pieces = ((integrals, xl), (first, second, d))
    with jax.named_scope("product"):
        theirs = [product(theirs_high, theirs_low, p) for p in pieces]
    with jax.named_scope("sum_core"):
        other = [swap(t, "core", 1) for t in theirs]
    with jax.named_scope("product"):
        sums = [product(ours_high, ours_low, pieces[0], other[0], (theirs[1],))]
        sums.append(product(ours_high, ours_low, pieces[1], other[1]))
    with jax.named_scope("sum_y"):
        got = [(swap(a, "y", 1), swap(b, "y", 3)) for a, _, b, _ in sums]
    halves = []
    for h in range(2):
        _, keep_a, _, keep_b = sums[h]
        got_a, got_b = got[h]
        with jax.named_scope("sum_y"):
            send_a, send_b = middle(keep_a, got_a, keep_b, got_b, after=(sums[1][0],) * (1 - h))
            last_a, last_b = swap(send_a, "y", 3), swap(send_b, "y", 1)
            own, up1, down1, across, two, six = finish(keep_a, got_a, last_a, keep_b, got_b, last_b)
        with jax.named_scope("to_owner"):
            across, up1, down1 = along_z(across, 4), along_z(up1, 7), along_z(down1, 1)
            up, down = pass_on(two, up1, six, down1, across)
            up, down = along_z(up, 6), along_z(down, 2)
            halves.append((own, up1, up, across, down, down1))
    with jax.named_scope("scale"):
        return scale(*halves, occ_energy, vir_energy)


def solution(mesh):
    split = Mesh(mesh.devices.reshape(SIZES), AXES)
    return jax.shard_map(
        on_device,
        mesh=split,
        in_specs=(P(PAIR, GRP, None), P(PAIR, GRP), P(), P(), P(), P(PAIR, GRP), P()),
        out_specs=P(PAIR, GRP, None),
        check_vma=False,
    )
```

```python
import jax
import jax.numpy as jnp
from jax import lax
from jax.experimental import pallas as pl
from jax.experimental.pallas import tpu as pltpu
from jax.sharding import Mesh, PartitionSpec as P

AXES = ("xl", "y", "core", "z", "xh")
SIZES = (2, 4, 2, 8, 2)
PAIR, GRP = ("xl", "y", "core"), ("z", "xh")
NZ = 8
CHEAP = pl.CostEstimate(flops=1000, bytes_accessed=1000, transcendentals=0)
VMEM = pl.BlockSpec(memory_space=pltpu.VMEM)
ANY = pl.BlockSpec(memory_space=pl.ANY)


def call(kernel, out_shape, operands, after=(), scratch=(), mib=8):
    several = isinstance(out_shape, list)

    def body(*refs):
        kernel(*refs[: len(operands)], *refs[len(operands) + len(after) :])

    return pl.pallas_call(
        body,
        out_shape=out_shape,
        in_specs=[VMEM] * len(operands) + [ANY] * len(after),
        out_specs=[VMEM] * len(out_shape) if several else VMEM,
        scratch_shapes=list(scratch),
        cost_estimate=CHEAP,
        compiler_params=pltpu.CompilerParams(vmem_limit_bytes=mib * 2**20),
        name=kernel.__name__,
    )(*operands, *after)


def f32(*shape):
    return jax.ShapeDtypeStruct(shape, jnp.float32)


def swap(x, axes, bits):
    names = axes if isinstance(axes, tuple) else (axes,)
    n = 1
    for a in names:
        n *= SIZES[AXES.index(a)]
    return lax.ppermute(x, axes, [(i, i ^ bits) for i in range(n)])


def along_z(x, d):
    return lax.ppermute(x, "z", [(i, (i + d) % NZ) for i in range(NZ)])


def mask_kernel(occ_ref, vir_ref, mask_ref, a_ref, near_ref, far_ref, held):
    xl, y, core = lax.axis_index("xl"), lax.axis_index("y"), lax.axis_index("core")
    z, xh = lax.axis_index("z"), lax.axis_index("xh")
    no, ni, width = a_ref.shape
    blocks = vir_ref.shape[0]
    part = width // 16
    col = lax.broadcasted_iota(jnp.int32, (1, width), 1)
    block = jnp.full((1, width), -1, jnp.int32)
    for s in range(blocks):
        block = block + (col >= vir_ref[s]).astype(jnp.int32)
    for oo in range(no):
        for ii in range(ni):
            o = ((xl * 4 + y) * 2 + core) * no + oo
            row = o * (ni * 16) + (z * 2 + xh) * ni + ii
            row_block = jnp.int32(-1)
            for s in range(occ_ref.shape[0]):
                row_block = row_block + (row >= occ_ref[s]).astype(jnp.int32)
            keep = jnp.zeros((1, width), jnp.float32)
            for v in range(blocks):
                keep = jnp.where(block == v, mask_ref[row_block, v].astype(jnp.float32), keep)
            held[oo * ni + ii : oo * ni + ii + 1, :] = a_ref[oo, ii : ii + 1, :] * keep
    for e in range(4):
        for dc in range(2):
            for dx in range(2):
                p = ((xl ^ dx) * 4 + (y ^ e)) * 2 + (core ^ dc)
                (near_ref, far_ref)[dc][e, :, dx * part : (dx + 1) * part] = held[
                    :, pl.ds(pl.multiple_of(p * part, part), part)
                ]


def mask_rows(amplitudes, occ_start, vir_start, block_mask):
    no, ni, width = amplitudes.shape
    smem = pl.BlockSpec(memory_space=pltpu.SMEM)
    half = jax.ShapeDtypeStruct((4, no * ni, width // 8), jnp.float32)
    return pl.pallas_call(
        mask_kernel,
        out_shape=[half, half],
        in_specs=[smem, smem, smem, VMEM],
        out_specs=[VMEM, VMEM],
        scratch_shapes=[pltpu.VMEM((no * ni, width), jnp.float32)],
        cost_estimate=CHEAP,
    )(occ_start, vir_start, block_mask, amplitudes)


def by_row_kernel(near_ref, far_ref, *outs):
    for e in range(4):
        outs[e][0] = near_ref[e]
        outs[e][1] = far_ref[e]


def by_row(near, far):
    return call(by_row_kernel, [f32(2, *near.shape[1:])] * 4, (near, far))


def line_up_kernel(*refs):
    rows, out_ref = refs[:4], refs[-1]
    nr = rows[0].shape[1]
    for dc in range(2):
        for e in range(4):
            at = (dc * 4 + e) * nr
            out_ref[at : at + nr, :] = rows[e][dc]


def line_up(rows):
    _, nr, depth = rows[0].shape
    return call(line_up_kernel, f32(8 * nr, depth), rows)


def relay_kernel(d1, u1, d2, u2, down, up):
    n = d1.shape[0]
    cut = down.shape[0] - n
    down[:n, :], down[n:, :] = d1[...], d2[:cut, :]
    up[:n, :], up[n:, :] = u1[...], u2[cut:, :]


def relay(d1, u1, d2, u2):
    n, depth = d1.shape
    cut = n // 16 * 8 + 8
    outs = [f32(n + cut, depth), f32(2 * n - cut, depth)]
    return call(relay_kernel, outs, (d1, u1, d2, u2))


def order_kernel(*refs):
    own, d1, u1, d2, u2, down, up = refs[:7]
    highs, lows, (held, across) = (refs[7], refs[9]), (refs[8], refs[10]), refs[11:]
    n = own.shape[0]
    nr = n // 8
    cut = down.shape[0] - n
    across[:cut, :] = down[n:, :]
    across[cut:, :] = up[n:, :]
    source = [(own, 0), (d1, 0), (d2, 0), (down, 0), (across, 0), (up, 0), (u2, 0), (u1, 0)]
    for dc in range(2):
        for e in range(4):
            for d, (ref, base) in enumerate(source):
                at = (e * NZ + d) * nr
                where = base + (dc * 4 + e) * nr
                held[at : at + nr, :] = ref[where : where + nr, :]
        value = held[...]
        high = value.astype(jnp.bfloat16)
        highs[dc][...] = high
        lows[dc][...] = (value - high.astype(jnp.float32)).astype(jnp.bfloat16)


def order_rows(*blocks):
    n, depth = blocks[0].shape
    part = jax.ShapeDtypeStruct((4 * n, depth), jnp.bfloat16)
    return call(order_kernel, [part] * 4, blocks, scratch=[pltpu.VMEM((k * n, depth), jnp.float32) for k in (4, 1)])


def halve_kernel(a, b, first, second):
    n = first.shape[0]
    first[...] = a[:n, :]
    second[...] = b[n:, :]


def halve(a, b, after):
    depth, width = a.shape
    return call(halve_kernel, [f32(depth // 2, width)] * 2, (a, b), after)


def three_passes(high_ref, low_ref, b_refs, cols, b_high, b_low):
    at = 0
    for ref in b_refs:
        value = ref[:, cols]
        high = value.astype(jnp.bfloat16)
        b_high[at : at + ref.shape[0], :] = high
        b_low[at : at + ref.shape[0], :] = (value - high.astype(jnp.float32)).astype(jnp.bfloat16)
        at += ref.shape[0]
    dot = lambda a, b: jnp.dot(a, b, preferred_element_type=jnp.float32)
    small = dot(high_ref[...], b_low[...]) + dot(low_ref[...], b_high[...])
    return small + dot(high_ref[...], b_high[...])


def theirs_kernel(high_ref, low_ref, *refs):
    b_refs, (out_ref, b_high, b_low) = refs[:-3], refs[-3:]
    width = b_high.shape[1]
    for s in range(2):
        cols = slice(s * width, (s + 1) * width)
        out_ref[:, cols] = three_passes(high_ref, low_ref, b_refs, cols, b_high, b_low)


def ours_kernel(high_ref, low_ref, *refs):
    b_refs, other_ref, outs, (b_high, b_low) = refs[:-7], refs[-7], refs[-6:-2], refs[-2:]
    width = b_high.shape[1]
    group = outs[0].shape[0] // 2
    for s in range(2):
        cols = slice(s * width, (s + 1) * width)
        value = three_passes(high_ref, low_ref, b_refs, cols, b_high, b_low) + other_ref[:, cols]
        part = [value[e * group : (e + 1) * group] for e in range(4)]
        send, keep = outs[2 * s], outs[2 * s + 1]
        gone, kept = (((1, 2), (0, 3)), ((2, 3), (0, 1)))[s]
        for k in range(2):
            send[k * group : (k + 1) * group, :] = part[gone[k]]
            keep[k * group : (k + 1) * group, :] = part[kept[k]]


def product(high, low, pieces, other=None, after=()):
    rows, depth = high.shape
    width = pieces[0].shape[1]
    scratch = [pltpu.VMEM((depth, width // 2), jnp.bfloat16)] * 2
    if other is None:
        return call(theirs_kernel, f32(rows, width), (high, low, *pieces), after, scratch, 16)
    outs = [f32(rows // 2, width // 2)] * 4
    return call(ours_kernel, outs, (high, low, *pieces, other), after, scratch, 16)


def middle_kernel(keep_a, got_a, keep_b, got_b, send_a, send_b):
    group = send_a.shape[0]
    send_a[...] = keep_a[group:, :] + got_a[group:, :]
    send_b[...] = keep_b[group:, :] + got_b[:group, :]


def middle(*args, after=()):
    n, width = args[0].shape
    return call(middle_kernel, [f32(n // 2, width)] * 2, args, after)


def finish_kernel(*refs):
    out_ref = refs[12]
    group, width = refs[2].shape
    nr = group // NZ
    z = lax.axis_index("z")
    for k in range(4):
        keep, got, last = refs[3 * k : 3 * k + 3]
        first = 0 if k % 2 == 0 else group
        value = keep[:group, :] + got[first : first + group, :] + last[...]
        for d in range(NZ):
            where = lax.rem(z + NZ - d, NZ)
            for j in range(width // 128):
                at = (k * (width // 128) + j) * nr
                tile = value[d * nr : (d + 1) * nr, j * 128 : (j + 1) * 128]
                out_ref[where, at : at + nr, :] = tile


def finish(*args):
    group, width = args[2].shape
    return call(finish_kernel, f32(NZ, 4 * width // 128 * (group // NZ), 128), args)


def scale_kernel(got_ref, occ_ref, vir_ref, out_ref):
    xh = lax.axis_index("xh")
    no, ni, _ = out_ref.shape
    nr = no * ni
    tiles = got_ref.shape[1] // (2 * nr)
    for d in range(NZ):
        for h in range(2):
            start = (d * 2 + (xh ^ h)) * tiles
            for j in range(tiles):
                at = (h * tiles + j) * nr
                cols = pl.ds(pl.multiple_of((start + j) * 128, 128), 128)
                value = got_ref[d, at : at + nr, :] / (occ_ref[...] - vir_ref[:, cols])
                for oo in range(no):
                    out_ref[oo, :, cols] = value[oo * ni : (oo + 1) * ni]


def scale(got, occ_energy, vir_energy):
    no, ni = occ_energy.shape
    operands = (got, occ_energy.reshape(no * ni, 1), vir_energy[None, :])
    return call(scale_kernel, f32(no, ni, vir_energy.shape[0]), operands)


def on_device(amplitudes, integrals, occ_start, vir_start, block_mask, occ_energy, vir_energy):
    with jax.named_scope("gather_integrals"):
        xl, d = swap(integrals, "xl", 1), swap(integrals, ("xl", "xh"), 3)
    with jax.named_scope("mask"):
        near, far = mask_rows(amplitudes, occ_start, vir_start, block_mask)
    with jax.named_scope("exchange_amplitudes"):
        pair = by_row(near, swap(far, "core", 1))
        rows = [pair[0]] + [swap(pair[e], "y", e) for e in (1, 2, 3)]
        mine = line_up(rows)
    with jax.named_scope("gather_amplitudes"):
        d2, u2 = along_z(mine, 2), along_z(mine, 6)
        d1, u1 = along_z(mine, 1), along_z(mine, 7)
        pairs = relay(d1, u1, d2, u2)
        down, up = along_z(pairs[0], 2), along_z(pairs[1], 6)
        parts = order_rows(mine, d1, u1, d2, u2, down, up)
        ours_high, ours_low, theirs_high, theirs_low = parts
    with jax.named_scope("gather_integrals"):
        first, second = halve(xl, d, after=(pairs[0],))
        first, second = swap(first, ("xl", "xh"), 3), swap(second, "xl", 1)
    pieces = ((integrals, xl), (first, second, d))
    with jax.named_scope("product"):
        theirs = [product(theirs_high, theirs_low, pieces[0])]
        theirs.append(product(theirs_high, theirs_low, pieces[1]))
    with jax.named_scope("sum_core"):
        other = [swap(t, "core", 1) for t in theirs]
    with jax.named_scope("product"):
        sums = [product(ours_high, ours_low, pieces[0], other[0], (theirs[1],))]
        sums.append(product(ours_high, ours_low, pieces[1], other[1]))
    with jax.named_scope("sum_y"):
        got = [(swap(a, "y", 1), swap(b, "y", 3)) for a, _, b, _ in sums]
    ends = []
    with jax.named_scope("sum_y"):
        for h in range(2):
            _, keep_a, _, keep_b = sums[h]
            got_a, got_b = got[h]
            send_a, send_b = middle(keep_a, got_a, keep_b, got_b, after=(sums[1][0],) * (1 - h))
            last_a, last_b = swap(send_a, "y", 3), swap(send_b, "y", 1)
            ends += [keep_a, got_a, last_a, keep_b, got_b, last_b]
        piece = finish(*ends)
    with jax.named_scope("to_owner"):
        piece = lax.all_to_all(piece, "z", split_axis=0, concat_axis=0, tiled=True)
    with jax.named_scope("scale"):
        return scale(piece, occ_energy, vir_energy)


def solution(mesh):
    split = Mesh(mesh.devices.reshape(SIZES), AXES)
    return jax.shard_map(
        on_device,
        mesh=split,
        in_specs=(P(PAIR, GRP, None), P(PAIR, GRP), P(), P(), P(), P(PAIR, GRP), P()),
        out_specs=P(PAIR, GRP, None),
        check_vma=False,
    )
```
